32 devices in a mesh: row: 8 (over y, x, core), col: 4 (over z).
Axes of the slice: x: 2, y: 2, z: 4, core: 2. Of those that a mesh axis runs over, the one named last changes fastest.
Arguments:
- density: bfloat16 [4096, 4096], P('row', 'col'), may hold values from -1.25 to 1.25, as said below
- hamiltonian: bfloat16 [4096, 4096], P('row', 'col'), may hold values from -60 to 60, as said below
- density_pattern: int32 [64, 64], replicated, may hold values from 0 to 1, as said below
- ham_pattern: int32 [64, 64], replicated, may hold values from 0 to 1, as said below
- source: int32 [64], replicated, may hold values from 0 to 63, as said below
Outputs:
- gradient: float32 [4096, 4096], P('row', 'col')
The draws below stay inside these ranges and needn't reach their ends.
Inputs may be any that keep to these rules, and one draw needn't show every extreme that they name: density is symmetric. hamiltonian is symmetric. `density_pattern`: symmetric, with ones on the diagonal. `ham_pattern`: symmetric, with ones on the diagonal. `source`: a permutation; cut the positions into panels of 8 in order, the last panel and the first being neighbours too: every block either keeps its position or trades it with a block of a neighbouring panel, and from one panel to a neighbouring one at most 2 blocks move, exactly 2 for some pair of panels.
All inputs are finite; a program needn't handle non-finite values.
Results may differ from the reference program's by a relative error of at most 0.0025.
Values may be sent and summed in bfloat16 or wider, within the bound.
A program may use at most 128 MiB of HBM per device.

```python
import math
import jax
import jax.numpy as jnp

BLK = 64
RB = 8
CAP = 2
NB = 64
NO = 4096


def symmetric_field(key, scale):
    first_key = jax.random.fold_in(key, 3)
    raw = jnp.clip(jax.random.normal(first_key, (NO, NO), jnp.float32), -4.0, 4.0)
    field = (raw + raw.T) * (scale / math.sqrt(2.0))
    return field


def symmetric_pattern(key):
    raw = jax.random.randint(key, (NB, NB), 0, 2, jnp.int32)
    symmetric = jnp.triu(raw) + jnp.triu(raw, 1).T
    return jnp.maximum(symmetric, jnp.eye(NB, dtype=jnp.int32))


def draw_density(key, part):
    return symmetric_field(jax.random.fold_in(key, 11), math.sqrt(2.0 / NO)).astype(jnp.bfloat16)


def draw_hamiltonian(key, part):
    return symmetric_field(jax.random.fold_in(key, 23), 1.0).astype(jnp.bfloat16)


def draw_density_pattern(key, part):
    return symmetric_pattern(jax.random.fold_in(key, 31))


def draw_ham_pattern(key, part):
    return symmetric_pattern(jax.random.fold_in(key, 47))


def panel_order(order_key):
    return jax.random.permutation(order_key, RB)


def draw_source(key, part):
    panels = NB // RB
    count_key = jax.random.fold_in(key, 53)
    forced_key = jax.random.fold_in(key, 59)
    order_key = jax.random.fold_in(key, 61)
    counts = jax.random.randint(count_key, (panels,), 1, CAP + 1, jnp.int32)
    forced = jax.random.randint(forced_key, (), 0, panels, jnp.int32)
    counts = jnp.where(jnp.arange(panels, dtype=jnp.int32) == forced, CAP, counts)
    orders = jax.vmap(panel_order)(jax.random.split(order_key, panels)).astype(jnp.int32)
    starts = jnp.arange(panels, dtype=jnp.int32) * RB
    nextup = jnp.roll(jnp.arange(panels, dtype=jnp.int32), -1)
    lower_side = starts[:, None] + orders[:, :CAP]
    upper_side = nextup[:, None] * RB + orders[nextup][:, CAP:2 * CAP]
    active = jnp.arange(CAP, dtype=jnp.int32)[None, :] < counts[:, None]
    lower_side = jnp.where(active, lower_side, NB).reshape(-1)
    upper_side = jnp.where(active, upper_side, NB).reshape(-1)
    mapping = jnp.arange(NB, dtype=jnp.int32)
    mapping = mapping.at[lower_side].set(upper_side, mode='drop')
    mapping = mapping.at[upper_side].set(lower_side, mode='drop')
    return mapping


def setup_inputs(seed: int = 0) -> dict:
    arg_keys = jax.random.split(jax.random.key(seed), 6)
    return {
        "density": draw_density(jax.random.fold_in(arg_keys[5], 71), 0),
        "hamiltonian": draw_hamiltonian(jax.random.fold_in(arg_keys[5], 71), 0),
        "density_pattern": draw_density_pattern(jax.random.fold_in(arg_keys[5], 71), 0),
        "ham_pattern": draw_ham_pattern(jax.random.fold_in(arg_keys[5], 71), 0),
        "source": draw_source(jax.random.fold_in(arg_keys[5], 71), 0),
    }


def apply_pattern(matrix, pattern):
    blocks = matrix.reshape(NB, BLK, NB, BLK)
    return (blocks * pattern[:, None, :, None].astype(matrix.dtype)).reshape(NB * BLK, NB * BLK)


def reference(density, hamiltonian, density_pattern, ham_pattern, source):
    blockwise = (source[:, None] * BLK + jnp.arange(BLK, dtype=jnp.int32)[None, :]).reshape(-1).astype(jnp.int32)
    moved = jnp.take(jnp.take(density, blockwise, axis=0), blockwise, axis=1)
    lnv = apply_pattern(moved, density_pattern)
    ham = apply_pattern(hamiltonian, ham_pattern)
    first = jnp.dot(lnv, ham, preferred_element_type=jnp.float32).astype(jnp.bfloat16)
    second = jnp.dot(lnv, first, preferred_element_type=jnp.float32)
    return 3.0 * first.astype(jnp.float32) - 2.0 * second
```

```python
import functools
import jax
import jax.numpy as jnp
from jax import lax
from jax.experimental import pallas as pl
from jax.experimental.pallas import tpu as pltpu
from jax.sharding import PartitionSpec as P

BLK = 64
CAP = 2
Q = 4
NT = 256
MESH = pl.DeviceIdType.MESH


def kernel(n, m, idx, den, ham, dmask, hmask, lanes, out, stack, pack, hfull, lbuf, fbuf, *rest):
    raws = rest[:Q]
    mig_s, mig_r, z_s, z_r, h_s, h_r, f_s, f_r = rest[Q:]
    me = lax.axis_index("row")
    zz = lax.axis_index("col")
    ext, _, width = den.shape
    rows = ext * BLK
    pairs = width // (2 * BLK)
    sub = rows // Q
    per = sub // BLK
    up, down = lax.rem(me + 1, n), lax.rem(me + n - 1, n)

    barrier = pltpu.get_barrier_semaphore()
    for p in range(1, n):
        pl.semaphore_signal(barrier, inc=1, device_id={"row": lax.rem(me + p, n)}, device_id_type=MESH)

    @pl.when(zz > 0)
    def _():
        pl.semaphore_signal(barrier, inc=1, device_id={"col": zz - 1}, device_id_type=MESH)

    @pl.when(zz < m - 1)
    def _():
        pl.semaphore_signal(barrier, inc=1, device_id={"col": zz + 1}, device_id_type=MESH)

    for side in range(2):
        for k in range(CAP):
            pack[side, k] = den[idx[side * CAP + k]]

    pl.semaphore_wait(barrier, n - 1 + (zz > 0).astype(jnp.int32) + (zz < m - 1).astype(jnp.int32))

    migrants = []
    for side, target in enumerate((up, down)):
        c = pltpu.make_async_remote_copy(
            src_ref=pack.at[side],
            dst_ref=stack.at[pl.ds(ext + side * CAP, CAP)],
            send_sem=mig_s.at[side],
            recv_sem=mig_r.at[side],
            device_id={"row": target},
            device_id_type=MESH,
        )
        c.start()
        migrants.append(c)

    for i in range(ext):
        s = pl.ds(i * BLK, BLK)
        hfull[me, s, :] = (ham[s, :].astype(jnp.float32) * hmask[pl.ds(i, 1), :]).astype(jnp.bfloat16)
    for i in range(ext):
        stack[i] = den[i]

    class Gather:
        def __init__(self, view, size, ss, rs):
            self.view, self.size, self.ss, self.rs = view, size, ss, rs
            self.sent = []
            y, x, k = me // 4, lax.rem(me // 2, 2), lax.rem(me, 2)
            self.X = y * 4 + (1 - x) * 2 + k
            self.Y = (1 - y) * 4 + x * 2 + k
            self.D = (1 - y) * 4 + (1 - x) * 2 + k
            self.C = y * 4 + x * 2 + (1 - k)
            self.half = size // 2

        def other(self, slot):
            return slot + 1 - 2 * lax.rem(slot, 2)

        def copy(self, idx, slot, lo, size, target):
            return pltpu.make_async_remote_copy(
                src_ref=self.view(slot, lo, size),
                dst_ref=self.view(slot, lo, size),
                send_sem=self.ss(idx),
                recv_sem=self.rs(idx),
                device_id={"row": target},
                device_id_type=MESH,
            )

        def send(self, *args):
            c = self.copy(*args)
            c.start()
            self.sent.append(c)

        def recv(self, idx, slot, lo, size):
            self.copy(idx, slot, lo, size, self.other(me) if n == 8 else up).wait_recv()

        def start(self):
            h, size = self.half, self.size
            if n != 8:
                for p in range(1, n):
                    self.send(p - 1, me, 0, size, lax.rem(me + p, n))
                return
            self.send(0, me, 0, h, self.X)
            self.send(3, me, h, h, self.Y)
            self.send(1, me, h, h, self.X)
            self.send(2, me, 0, h, self.Y)
            self.send(6, me, 0, size, self.C)

        def turn(self):
            if n != 8:
                return
            h = self.half
            self.recv(0, self.X, 0, h)
            self.send(4, self.X, 0, h, self.Y)
            self.recv(3, self.Y, h, h)
            self.send(5, self.Y, h, h, self.X)

        def share(self):
            if n != 8:
                return
            h, size = self.half, self.size
            self.recv(1, self.X, h, h)
            self.send(7, self.X, 0, size, self.C)
            self.recv(2, self.Y, 0, h)
            self.send(8, self.Y, 0, size, self.C)

        def finish(self):
            h, size = self.half, self.size
            if n != 8:
                for p in range(1, n):
                    self.recv(p - 1, lax.rem(me + n - p, n), 0, size)
                return
            self.recv(4, self.D, 0, h)
            self.recv(5, self.D, h, h)
            self.send(9, self.D, 0, size, self.C)
            for idx, slot in ((6, self.C), (7, self.other(self.X)), (8, self.other(self.Y)), (9, self.other(self.D))):
                self.recv(idx, slot, 0, size)

        def drain(self):
            for c in self.sent:
                c.wait_send()

    gh = Gather(lambda s, lo, size: hfull.at[s, pl.ds(lo, size), :], rows, lambda i: h_s.at[i], lambda i: h_r.at[i])
    gh.start()

    for c in migrants:
        c.wait_recv()
    for i in range(ext):
        block = stack[idx[2 * CAP + i]]
        for t in range(pairs):
            raws[i // per][zz * pairs + t, pl.ds((i % per) * BLK, BLK), :] = block[:, t * 2 * BLK:(t + 1) * 2 * BLK]

    def zcopy(d, q, dist, tile):
        ref = raws[q].at[pl.ds(tile * pairs, pairs)]
        return pltpu.make_async_remote_copy(
            src_ref=ref,
            dst_ref=ref,
            send_sem=z_s.at[d, q, dist],
            recv_sem=z_r.at[d, q, dist],
            device_id={"col": zz - 1 if d == 0 else zz + 1},
            device_id_type=MESH,
        )

    def zown(q):
        for d in range(2):
            @pl.when(zz > 0 if d == 0 else zz < m - 1)
            def _():
                zcopy(d, q, 0, zz).start()

    def zstep(q, dist):
        for d in range(2):
            tile = zz + dist if d == 0 else zz - dist
            there = tile < m if d == 0 else tile >= 0

            @pl.when(there)
            def _():
                zcopy(d, q, dist - 1, tile).wait_recv()

            if dist < m - 1:
                @pl.when(there & (zz > 0 if d == 0 else zz < m - 1))
                def _():
                    zcopy(d, q, dist, tile).start()

    def zdrain():
        for q in range(Q):
            for d in range(2):
                for dist in range(m - 1):
                    tile = zz + dist if d == 0 else zz - dist
                    there = (tile < m if d == 0 else tile >= 0) & (zz > 0 if d == 0 else zz < m - 1)

                    @pl.when(there)
                    def _():
                        zcopy(d, q, dist, tile).wait_send()

    def order(q):
        for c in range(Q):
            @pl.loop(0, n)
            def _(r):
                j = 2 * CAP + ext + r * ext + c * per
                a = raws[q][idx[j]].astype(jnp.float32)
                b = raws[q][idx[j + 1]].astype(jnp.float32)
                cols = pl.ds(pl.multiple_of(r * sub, sub), sub)
                v = a * lanes[c, 0:1, cols] + pltpu.roll(a, BLK, 1) * lanes[c, 1:2, cols]
                v += pltpu.roll(b, BLK, 1) * lanes[c, 2:3, cols] + b * lanes[c, 3:4, cols]
                for i in range(per):
                    w = v[i * BLK:(i + 1) * BLK] * dmask[c, pl.ds(q * per + i, 1), cols]
                    lbuf[c, pl.ds(q * sub + i * BLK, BLK), cols] = w.astype(jnp.bfloat16)

    def first(q):
        @pl.loop(0, width // NT)
        def _(t):
            cols = pl.ds(pl.multiple_of(t * NT, NT), NT)
            total = jnp.zeros((sub, NT), jnp.float32)
            for c in range(Q):
                h = hfull[:, pl.ds(c * sub, sub), cols].reshape(n * sub, NT)
                total += jnp.dot(lbuf[c, pl.ds(q * sub, sub), :], h, preferred_element_type=jnp.float32)
            fbuf[q, me, :, cols] = total.astype(jnp.bfloat16)

    def second(q):
        @pl.loop(0, width // NT)
        def _(t):
            cols = pl.ds(pl.multiple_of(t * NT, NT), NT)
            f = fbuf[q, :, :, cols].reshape(n * sub, NT)
            total = jnp.dot(lbuf[q], f, preferred_element_type=jnp.float32)
            if q > 0:
                total += out[:, cols]
            if q == Q - 1:
                own = fbuf[:, me, :, cols].reshape(rows, NT).astype(jnp.float32)
                total = 3.0 * own - 2.0 * total
            out[:, cols] = total

    gf = [
        Gather(
            (lambda q: lambda s, lo, size: fbuf.at[q, s, pl.ds(lo, size), :])(q),
            sub,
            (lambda q: lambda i: f_s.at[q, i])(q),
            (lambda q: lambda i: f_r.at[q, i])(q),
        )
        for q in range(Q)
    ]

    zown(0)
    zown(1)
    zstep(0, 1)
    gh.turn()
    for dist in range(2, m):
        zstep(0, dist)
    zown(2)
    zstep(1, 1)
    order(0)
    gh.share()
    for dist in range(2, m):
        zstep(1, dist)
    zown(3)
    zstep(2, 1)
    order(1)
    gh.finish()
    first(0)
    gf[0].start()
    first(1)
    gf[1].start()
    gf[0].turn()
    for dist in range(2, m):
        zstep(2, dist)
    zstep(3, 1)
    order(2)
    first(2)
    gf[2].start()
    gf[1].turn()
    gf[0].share()
    gf[0].finish()
    gf[1].share()
    gf[1].finish()
    gf[2].turn()
    for dist in range(2, m):
        zstep(3, dist)
    order(3)
    first(3)
    gf[3].start()
    gf[2].share()
    second(0)
    gf[3].turn()
    gf[2].finish()
    second(1)
    gf[3].share()
    second(2)
    gf[3].finish()
    second(3)

    for c in migrants:
        c.wait_send()
    zdrain()
    gh.drain()
    for g in gf:
        g.drain()


def body(density, hamiltonian, density_pattern, ham_pattern, source):
    n, m = lax.axis_size("row"), lax.axis_size("col")
    rows, width = density.shape
    ext, wide = rows // BLK, width // BLK
    per = ext // Q
    sub = rows // Q
    me, zz = lax.axis_index("row"), lax.axis_index("col")
    rp = lax.dynamic_slice_in_dim(density_pattern, me * ext, ext, 0).astype(jnp.float32)
    rp = rp.reshape(ext, n, Q, per).transpose(2, 0, 1, 3)
    dmask = jnp.broadcast_to(rp[..., None], (Q, ext, n, per, BLK)).reshape(Q, ext, n * sub)
    hp = lax.dynamic_slice(ham_pattern, (me * ext, zz * wide), (ext, wide)).astype(jnp.float32)
    hmask = jnp.broadcast_to(hp[..., None], (ext, wide, BLK)).reshape(ext, width)
    places = jnp.arange(ext, dtype=jnp.int32)
    up, down = (me + 1) % n, (me - 1) % n

    def mine(target):
        return lax.dynamic_slice_in_dim(source, target * ext, ext)

    def rank(hit):
        before = places[None, :] < places[:, None]
        return jnp.sum(jnp.where(before & hit[None, :], 1, 0), axis=1)

    picks = []
    for target in (up, down):
        olds = mine(target)
        hit = olds // ext == me
        order = rank(hit)
        for k in range(CAP):
            picks.append(jnp.sum(jnp.where(hit & (order == k), olds % ext, 0)).reshape(1))
    olds = mine(me)
    lower, upper = olds // ext == down, olds // ext == up
    assembled = jnp.where(
        lower, ext + rank(lower), jnp.where(upper, ext + CAP + rank(upper), olds % ext)
    )
    idx = jnp.concatenate(picks + [assembled, source // 2]).astype(jnp.int32)
    odd = (source % 2).astype(jnp.float32).reshape(n, Q, per).transpose(1, 0, 2)
    zero = jnp.zeros_like(odd[..., 0])
    halves = [
        (1 - odd[..., 0], zero),
        (odd[..., 0], zero),
        (zero, 1 - odd[..., 1]),
        (zero, odd[..., 1]),
    ]
    lanes = jnp.stack([jnp.stack(h, axis=-1) for h in halves], axis=1)
    lanes = jnp.broadcast_to(lanes[..., None], lanes.shape + (BLK,)).reshape(Q, 4, n * sub)
    sems = max(10, n - 1)
    dma = pltpu.SemaphoreType.DMA
    bf = jnp.bfloat16
    vm = pl.BlockSpec(memory_space=pltpu.VMEM)
    return pl.pallas_call(
        functools.partial(kernel, n, m),
        out_shape=jax.ShapeDtypeStruct((rows, width), jnp.float32),
        in_specs=[pl.BlockSpec(memory_space=pltpu.SMEM), vm, vm, vm, vm, vm],
        out_specs=vm,
        scratch_shapes=[
            pltpu.VMEM((ext + 2 * CAP, BLK, width), bf),
            pltpu.VMEM((2, CAP, BLK, width), bf),
            pltpu.VMEM((n, rows, width), bf),
            pltpu.VMEM((Q, rows, n * sub), bf),
            pltpu.VMEM((Q, n, sub, width), bf),
        ]
        + [pltpu.VMEM((m * width // (2 * BLK), sub, 2 * BLK), bf) for _ in range(Q)]
        + [
            dma((2,)), dma((2,)),
            dma((2, Q, m)), dma((2, Q, m)),
            dma((sems,)), dma((sems,)),
            dma((Q, sems)), dma((Q, sems)),
        ],
        compiler_params=pltpu.CompilerParams(
            collective_id=0, has_side_effects=True, vmem_limit_bytes=(60 if n > 8 else 48) * 1024 * 1024
        ),
        cost_estimate=pl.CostEstimate(
            flops=4 * rows * n * rows * width, bytes_accessed=8 * rows * width, transcendentals=0
        ),
    )(idx, density.reshape(ext, BLK, width), hamiltonian, dmask, hmask, lanes)


def solution(mesh):
    return jax.shard_map(
        body,
        mesh=mesh,
        in_specs=(P("row", "col"), P("row", "col"), P(), P(), P()),
        out_specs=P("row", "col"),
        check_vma=False,
    )
```

```python
import functools
import jax
import jax.numpy as jnp
from jax import lax
from jax.experimental import pallas as pl
from jax.experimental.pallas import tpu as pltpu
from jax.sharding import PartitionSpec as P

BLK = 64
CAP = 2
Q = 4
NT = 256
MESH = pl.DeviceIdType.MESH


def kernel(n, m, src, dpat, hpat, den, ham, out, stack, pack, hfull, lbuf, fbuf, *rest):
    raws = rest[:Q]
    mig_s, mig_r, z_s, z_r, h_s, h_r, f_s, f_r = rest[Q:]
    me = lax.axis_index("row")
    zz = lax.axis_index("col")
    ext, _, width = den.shape
    rows = ext * BLK
    pairs = width // (2 * BLK)
    sub = rows // Q
    per = sub // BLK
    up, down = lax.rem(me + 1, n), lax.rem(me + n - 1, n)

    barrier = pltpu.get_barrier_semaphore()
    for p in range(1, n):
        pl.semaphore_signal(barrier, inc=1, device_id={"row": lax.rem(me + p, n)}, device_id_type=MESH)

    @pl.when(zz > 0)
    def _():
        pl.semaphore_signal(barrier, inc=1, device_id={"col": zz - 1}, device_id_type=MESH)

    @pl.when(zz < m - 1)
    def _():
        pl.semaphore_signal(barrier, inc=1, device_id={"col": zz + 1}, device_id_type=MESH)

    for side, target in enumerate((up, down)):
        count = jnp.int32(0)
        picks = [jnp.int32(0)] * CAP
        for i in range(ext):
            a = src[target * ext + i]
            hit = (lax.div(a, ext) == me).astype(jnp.int32)
            for k in range(CAP):
                picks[k] = picks[k] + hit * (count == k).astype(jnp.int32) * lax.rem(a, ext)
            count = count + hit
        for k in range(CAP):
            pack[side, k] = den[picks[k]]

    pl.semaphore_wait(barrier, n - 1 + (zz > 0).astype(jnp.int32) + (zz < m - 1).astype(jnp.int32))

    migrants = []
    for side, target in enumerate((up, down)):
        c = pltpu.make_async_remote_copy(
            src_ref=pack.at[side],
            dst_ref=stack.at[pl.ds(ext + side * CAP, CAP)],
            send_sem=mig_s.at[side],
            recv_sem=mig_r.at[side],
            device_id={"row": target},
            device_id_type=MESH,
        )
        c.start()
        migrants.append(c)

    lane = lax.broadcasted_iota(jnp.int32, (1, 2 * BLK), 1)
    low = (lane < BLK).astype(jnp.float32)
    high = 1.0 - low

    def keep(p0, p1):
        return low * p0.astype(jnp.float32) + high * p1.astype(jnp.float32)

    @pl.loop(0, ext)
    def _(i):
        for t in range(pairs):
            j = zz * pairs * 2 + t * 2
            s = pl.ds(pl.multiple_of(i * BLK, BLK), BLK)
            cols = pl.ds(t * 2 * BLK, 2 * BLK)
            row = me * ext + i
            w = ham[s, cols].astype(jnp.float32) * keep(hpat[row, j], hpat[row, j + 1])
            hfull[me, s, cols] = w.astype(jnp.bfloat16)

    for i in range(ext):
        stack[i] = den[i]

    class Gather:
        def __init__(self, view, size, ss, rs):
            self.view, self.size, self.ss, self.rs = view, size, ss, rs
            self.sent = []
            y, x, k = me // 4, lax.rem(me // 2, 2), lax.rem(me, 2)
            self.X = y * 4 + (1 - x) * 2 + k
            self.Y = (1 - y) * 4 + x * 2 + k
            self.D = (1 - y) * 4 + (1 - x) * 2 + k
            self.C = y * 4 + x * 2 + (1 - k)
            self.half = size // 2

        def other(self, slot):
            return slot + 1 - 2 * lax.rem(slot, 2)

        def copy(self, idx, slot, lo, size, target):
            return pltpu.make_async_remote_copy(
                src_ref=self.view(slot, lo, size),
                dst_ref=self.view(slot, lo, size),
                send_sem=self.ss(idx),
                recv_sem=self.rs(idx),
                device_id={"row": target},
                device_id_type=MESH,
            )

        def send(self, *args):
            c = self.copy(*args)
            c.start()
            self.sent.append(c)

        def recv(self, idx, slot, lo, size):
            self.copy(idx, slot, lo, size, self.other(me) if n == 8 else up).wait_recv()

        def start(self):
            h, size = self.half, self.size
            if n != 8:
                for p in range(1, n):
                    self.send(p - 1, me, 0, size, lax.rem(me + p, n))
                return
            self.send(0, me, 0, h, self.X)
            self.send(3, me, h, h, self.Y)
            self.send(1, me, h, h, self.X)
            self.send(2, me, 0, h, self.Y)
            self.send(6, me, 0, size, self.C)

        def turn(self):
            if n != 8:
                return
            h = self.half
            self.recv(0, self.X, 0, h)
            self.send(4, self.X, 0, h, self.Y)
            self.recv(3, self.Y, h, h)
            self.send(5, self.Y, h, h, self.X)

        def share(self):
            if n != 8:
                return
            h, size = self.half, self.size
            self.recv(1, self.X, h, h)
            self.send(7, self.X, 0, size, self.C)
            self.recv(2, self.Y, 0, h)
            self.send(8, self.Y, 0, size, self.C)

        def finish(self):
            h, size = self.half, self.size
            if n != 8:
                for p in range(1, n):
                    self.recv(p - 1, lax.rem(me + n - p, n), 0, size)
                return
            self.recv(4, self.D, 0, h)
            self.recv(5, self.D, h, h)
            self.send(9, self.D, 0, size, self.C)
            for idx, slot in ((6, self.C), (7, self.other(self.X)), (8, self.other(self.Y)), (9, self.other(self.D))):
                self.recv(idx, slot, 0, size)

        def drain(self):
            for c in self.sent:
                c.wait_send()

    gh = Gather(lambda s, lo, size: hfull.at[s, pl.ds(lo, size), :], rows, lambda i: h_s.at[i], lambda i: h_r.at[i])
    gh.start()

    for c in migrants:
        c.wait_recv()
    nlow, nupp = jnp.int32(0), jnp.int32(0)
    for i in range(ext):
        a = src[me * ext + i]
        home = lax.div(a, ext)
        lower, upper = (home == down).astype(jnp.int32), (home == up).astype(jnp.int32)
        pick = lower * (ext + jnp.minimum(nlow, CAP - 1)) + upper * (ext + CAP + jnp.minimum(nupp, CAP - 1)) + (1 - lower - upper) * lax.rem(a, ext)
        nlow = nlow + lower
        nupp = nupp + upper
        block = stack[pick]
        for t in range(pairs):
            raws[i // per][zz * pairs + t, pl.ds((i % per) * BLK, BLK), :] = block[:, t * 2 * BLK:(t + 1) * 2 * BLK]

    def zcopy(d, q, dist, tile):
        ref = raws[q].at[pl.ds(tile * pairs, pairs)]
        return pltpu.make_async_remote_copy(
            src_ref=ref,
            dst_ref=ref,
            send_sem=z_s.at[d, q, dist],
            recv_sem=z_r.at[d, q, dist],
            device_id={"col": zz - 1 if d == 0 else zz + 1},
            device_id_type=MESH,
        )

    def zown(q):
        for d in range(2):
            @pl.when(zz > 0 if d == 0 else zz < m - 1)
            def _():
                zcopy(d, q, 0, zz).start()

    def zstep(q, dist):
        for d in range(2):
            tile = zz + dist if d == 0 else zz - dist
            there = tile < m if d == 0 else tile >= 0

            @pl.when(there)
            def _():
                zcopy(d, q, dist - 1, tile).wait_recv()

            if dist < m - 1:
                @pl.when(there & (zz > 0 if d == 0 else zz < m - 1))
                def _():
                    zcopy(d, q, dist, tile).start()

    def zdrain():
        for q in range(Q):
            for d in range(2):
                for dist in range(m - 1):
                    tile = zz + dist if d == 0 else zz - dist
                    there = (tile < m if d == 0 else tile >= 0) & (zz > 0 if d == 0 else zz < m - 1)

                    @pl.when(there)
                    def _():
                        zcopy(d, q, dist, tile).wait_send()

    def order(q):
        for c in range(Q):
            @pl.loop(0, n)
            def _(r):
                j = r * ext + c * per
                s0, s1 = src[j], src[j + 1]
                e0, e1 = lax.rem(s0, 2).astype(jnp.float32), lax.rem(s1, 2).astype(jnp.float32)
                a = raws[q][lax.div(s0, 2)].astype(jnp.float32)
                b = raws[q][lax.div(s1, 2)].astype(jnp.float32)
                cols = pl.ds(pl.multiple_of(r * sub, sub), sub)
                v = a * (low * (1.0 - e0)) + pltpu.roll(a, BLK, 1) * (low * e0)
                v += pltpu.roll(b, BLK, 1) * (high * (1.0 - e1)) + b * (high * e1)
                for i in range(per):
                    row = me * ext + q * per + i
                    w = v[i * BLK:(i + 1) * BLK] * keep(dpat[row, j], dpat[row, j + 1])
                    lbuf[c, pl.ds(q * sub + i * BLK, BLK), cols] = w.astype(jnp.bfloat16)

    def first(q):
        @pl.loop(0, width // NT)
        def _(t):
            cols = pl.ds(pl.multiple_of(t * NT, NT), NT)
            total = jnp.zeros((sub, NT), jnp.float32)
            for c in range(Q):
                h = hfull[:, pl.ds(c * sub, sub), cols].reshape(n * sub, NT)
                total += jnp.dot(lbuf[c, pl.ds(q * sub, sub), :], h, preferred_element_type=jnp.float32)
            fbuf[q, me, :, cols] = total.astype(jnp.bfloat16)

    def second(q):
        @pl.loop(0, width // NT)
        def _(t):
            cols = pl.ds(pl.multiple_of(t * NT, NT), NT)
            f = fbuf[q, :, :, cols].reshape(n * sub, NT)
            total = jnp.dot(lbuf[q], f, preferred_element_type=jnp.float32)
            if q > 0:
                total += out[:, cols]
            if q == Q - 1:
                own = fbuf[:, me, :, cols].reshape(rows, NT).astype(jnp.float32)
                total = 3.0 * own - 2.0 * total
            out[:, cols] = total

    gf = [
        Gather(
            (lambda q: lambda s, lo, size: fbuf.at[q, s, pl.ds(lo, size), :])(q),
            sub,
            (lambda q: lambda i: f_s.at[q, i])(q),
            (lambda q: lambda i: f_r.at[q, i])(q),
        )
        for q in range(Q)
    ]

    zown(0)
    zown(1)
    zstep(0, 1)
    gh.turn()
    for dist in range(2, m):
        zstep(0, dist)
    zown(2)
    zstep(1, 1)
    order(0)
    gh.share()
    for dist in range(2, m):
        zstep(1, dist)
    zown(3)
    zstep(2, 1)
    order(1)
    gh.finish()
    first(0)
    gf[0].start()
    first(1)
    gf[1].start()
    gf[0].turn()
    for dist in range(2, m):
        zstep(2, dist)
    zstep(3, 1)
    order(2)
    first(2)
    gf[2].start()
    gf[1].turn()
    gf[0].share()
    gf[0].finish()
    gf[1].share()
    gf[1].finish()
    gf[2].turn()
    for dist in range(2, m):
        zstep(3, dist)
    order(3)
    first(3)
    gf[3].start()
    gf[2].share()
    second(0)
    gf[3].turn()
    gf[2].finish()
    second(1)
    gf[3].share()
    second(2)
    gf[3].finish()
    second(3)

    for c in migrants:
        c.wait_send()
    zdrain()
    gh.drain()
    for g in gf:
        g.drain()


def body(density, hamiltonian, density_pattern, ham_pattern, source):
    n, m = lax.axis_size("row"), lax.axis_size("col")
    rows, width = density.shape
    ext = rows // BLK
    sub = rows // Q
    sems = max(10, n - 1)
    dma = pltpu.SemaphoreType.DMA
    bf = jnp.bfloat16
    sm = pl.BlockSpec(memory_space=pltpu.SMEM)
    vm = pl.BlockSpec(memory_space=pltpu.VMEM)
    return pl.pallas_call(
        functools.partial(kernel, n, m),
        out_shape=jax.ShapeDtypeStruct((rows, width), jnp.float32),
        in_specs=[sm, sm, sm, vm, vm],
        out_specs=vm,
        scratch_shapes=[
            pltpu.VMEM((ext + 2 * CAP, BLK, width), bf),
            pltpu.VMEM((2, CAP, BLK, width), bf),
            pltpu.VMEM((n, rows, width), bf),
            pltpu.VMEM((Q, rows, n * sub), bf),
            pltpu.VMEM((Q, n, sub, width), bf),
        ]
        + [pltpu.VMEM((m * width // (2 * BLK), sub, 2 * BLK), bf) for _ in range(Q)]
        + [
            dma((2,)), dma((2,)),
            dma((2, Q, m)), dma((2, Q, m)),
            dma((sems,)), dma((sems,)),
            dma((Q, sems)), dma((Q, sems)),
        ],
        compiler_params=pltpu.CompilerParams(
            collective_id=0, has_side_effects=True, vmem_limit_bytes=(60 if n > 8 else 48) * 1024 * 1024
        ),
        cost_estimate=pl.CostEstimate(
            flops=4 * rows * n * rows * width, bytes_accessed=8 * rows * width, transcendentals=0
        ),
    )(source, density_pattern, ham_pattern, density.reshape(ext, BLK, width), hamiltonian)


def solution(mesh):
    return jax.shard_map(
        body,
        mesh=mesh,
        in_specs=(P("row", "col"), P("row", "col"), P(), P(), P()),
        out_specs=P("row", "col"),
        check_vma=False,
    )
```

```python
import functools
import jax
import jax.numpy as jnp
from jax import lax
from jax.experimental import pallas as pl
from jax.experimental.pallas import tpu as pltpu
from jax.sharding import PartitionSpec as P

BLK = 64
CAP = 2
Q = 4
NT = 256
MESH = pl.DeviceIdType.MESH


def kernel(n, m, src, dpat, hpat, den_hbm, ham_hbm, out, den, ham, stack, pack, hfull, lbuf, fbuf, *rest):
    raws = rest[:Q]
    mig_s, mig_r, z_s, z_r, h_s, h_r, f_s, f_r, in_s = rest[Q:]
    me = lax.axis_index("row")
    zz = lax.axis_index("col")
    ext, _, width = den.shape
    rows = ext * BLK
    pairs = width // (2 * BLK)
    sub = rows // Q
    per = sub // BLK
    up, down = lax.rem(me + 1, n), lax.rem(me + n - 1, n)
    loads = [
        pltpu.make_async_copy(den_hbm, den, in_s.at[0]),
        pltpu.make_async_copy(ham_hbm, ham, in_s.at[1]),
        pltpu.make_async_copy(den_hbm, stack.at[pl.ds(0, ext)], in_s.at[2]),
    ]
    for c in loads:
        c.start()

    barrier = pltpu.get_barrier_semaphore()
    for p in range(1, n):
        pl.semaphore_signal(barrier, inc=1, device_id={"row": lax.rem(me + p, n)}, device_id_type=MESH)

    @pl.when(zz > 0)
    def _():
        pl.semaphore_signal(barrier, inc=1, device_id={"col": zz - 1}, device_id_type=MESH)

    @pl.when(zz < m - 1)
    def _():
        pl.semaphore_signal(barrier, inc=1, device_id={"col": zz + 1}, device_id_type=MESH)

    loads[0].wait()
    for side, target in enumerate((up, down)):
        count = jnp.int32(0)
        picks = [jnp.int32(0)] * CAP
        for i in range(ext):
            a = src[target * ext + i]
            hit = (lax.div(a, ext) == me).astype(jnp.int32)
            for k in range(CAP):
                picks[k] = picks[k] + hit * (count == k).astype(jnp.int32) * lax.rem(a, ext)
            count = count + hit
        for k in range(CAP):
            pack[side, k] = den[picks[k]]

    pl.semaphore_wait(barrier, n - 1 + (zz > 0).astype(jnp.int32) + (zz < m - 1).astype(jnp.int32))

    migrants = []
    for side, target in enumerate((up, down)):
        c = pltpu.make_async_remote_copy(
            src_ref=pack.at[side],
            dst_ref=stack.at[pl.ds(ext + side * CAP, CAP)],
            send_sem=mig_s.at[side],
            recv_sem=mig_r.at[side],
            device_id={"row": target},
            device_id_type=MESH,
        )
        c.start()
        migrants.append(c)

    loads[1].wait()
    lane = lax.broadcasted_iota(jnp.int32, (1, 2 * BLK), 1)
    low = (lane < BLK).astype(jnp.float32)
    high = 1.0 - low

    def keep(p0, p1):
        return low * p0.astype(jnp.float32) + high * p1.astype(jnp.float32)

    @pl.loop(0, ext)
    def _(i):
        for t in range(pairs):
            j = zz * pairs * 2 + t * 2
            s = pl.ds(pl.multiple_of(i * BLK, BLK), BLK)
            cols = pl.ds(t * 2 * BLK, 2 * BLK)
            row = me * ext + i
            w = ham[s, cols].astype(jnp.float32) * keep(hpat[row, j], hpat[row, j + 1])
            hfull[me, s, cols] = w.astype(jnp.bfloat16)

    loads[2].wait()

    class Gather:
        def __init__(self, view, size, ss, rs):
            self.view, self.size, self.ss, self.rs = view, size, ss, rs
            self.sent = []
            y, x, k = me // 4, lax.rem(me // 2, 2), lax.rem(me, 2)
            self.X = y * 4 + (1 - x) * 2 + k
            self.Y = (1 - y) * 4 + x * 2 + k
            self.D = (1 - y) * 4 + (1 - x) * 2 + k
            self.C = y * 4 + x * 2 + (1 - k)
            self.half = size // 2

        def other(self, slot):
            return slot + 1 - 2 * lax.rem(slot, 2)

        def copy(self, idx, slot, lo, size, target):
            return pltpu.make_async_remote_copy(
                src_ref=self.view(slot, lo, size),
                dst_ref=self.view(slot, lo, size),
                send_sem=self.ss(idx),
                recv_sem=self.rs(idx),
                device_id={"row": target},
                device_id_type=MESH,
            )

        def send(self, *args):
            c = self.copy(*args)
            c.start()
            self.sent.append(c)

        def recv(self, idx, slot, lo, size):
            self.copy(idx, slot, lo, size, self.other(me) if n == 8 else up).wait_recv()

        def start(self):
            h, size = self.half, self.size
            if n != 8:
                for p in range(1, n):
                    self.send(p - 1, me, 0, size, lax.rem(me + p, n))
                return
            self.send(0, me, 0, h, self.X)
            self.send(3, me, h, h, self.Y)
            self.send(1, me, h, h, self.X)
            self.send(2, me, 0, h, self.Y)
            self.send(6, me, 0, size, self.C)

        def turn(self):
            if n != 8:
                return
            h = self.half
            self.recv(0, self.X, 0, h)
            self.send(4, self.X, 0, h, self.Y)
            self.recv(3, self.Y, h, h)
            self.send(5, self.Y, h, h, self.X)

        def share(self):
            if n != 8:
                return
            h, size = self.half, self.size
            self.recv(1, self.X, h, h)
            self.send(7, self.X, 0, size, self.C)
            self.recv(2, self.Y, 0, h)
            self.send(8, self.Y, 0, size, self.C)

        def finish(self):
            h, size = self.half, self.size
            if n != 8:
                for p in range(1, n):
                    self.recv(p - 1, lax.rem(me + n - p, n), 0, size)
                return
            self.recv(4, self.D, 0, h)
            self.send(9, self.D, 0, h, self.C)
            self.recv(5, self.D, h, h)
            self.send(10, self.D, h, h, self.C)
            for idx, slot in ((6, self.C), (7, self.other(self.X)), (8, self.other(self.Y))):
                self.recv(idx, slot, 0, size)
            self.recv(9, self.other(self.D), 0, h)
            self.recv(10, self.other(self.D), h, h)

        def drain(self):
            for c in self.sent:
                c.wait_send()

    gh = Gather(lambda s, lo, size: hfull.at[s, pl.ds(lo, size), :], rows, lambda i: h_s.at[i], lambda i: h_r.at[i])
    gh.start()

    for c in migrants:
        c.wait_recv()
    nlow, nupp = jnp.int32(0), jnp.int32(0)
    for i in range(ext):
        a = src[me * ext + i]
        home = lax.div(a, ext)
        lower, upper = (home == down).astype(jnp.int32), (home == up).astype(jnp.int32)
        pick = lower * (ext + jnp.minimum(nlow, CAP - 1)) + upper * (ext + CAP + jnp.minimum(nupp, CAP - 1)) + (1 - lower - upper) * lax.rem(a, ext)
        nlow = nlow + lower
        nupp = nupp + upper
        block = stack[pick]
        for t in range(pairs):
            raws[i // per][zz * pairs + t, pl.ds((i % per) * BLK, BLK), :] = block[:, t * 2 * BLK:(t + 1) * 2 * BLK]

    def zcopy(d, q, dist, tile):
        ref = raws[q].at[pl.ds(tile * pairs, pairs)]
        return pltpu.make_async_remote_copy(
            src_ref=ref,
            dst_ref=ref,
            send_sem=z_s.at[d, q, dist],
            recv_sem=z_r.at[d, q, dist],
            device_id={"col": zz - 1 if d == 0 else zz + 1},
            device_id_type=MESH,
        )

    def zown(q):
        for d in range(2):
            @pl.when(zz > 0 if d == 0 else zz < m - 1)
            def _():
                zcopy(d, q, 0, zz).start()

    def zstep(q, dist):
        for d in range(2):
            tile = zz + dist if d == 0 else zz - dist
            there = tile < m if d == 0 else tile >= 0

            @pl.when(there)
            def _():
                zcopy(d, q, dist - 1, tile).wait_recv()

            if dist < m - 1:
                @pl.when(there & (zz > 0 if d == 0 else zz < m - 1))
                def _():
                    zcopy(d, q, dist, tile).start()

    def zdrain():
        for q in range(Q):
            for d in range(2):
                for dist in range(m - 1):
                    tile = zz + dist if d == 0 else zz - dist
                    there = (tile < m if d == 0 else tile >= 0) & (zz > 0 if d == 0 else zz < m - 1)

                    @pl.when(there)
                    def _():
                        zcopy(d, q, dist, tile).wait_send()

    def order(q):
        for c in range(Q):
            @pl.loop(0, n)
            def _(r):
                j = r * ext + c * per
                s0, s1 = src[j], src[j + 1]
                e0, e1 = lax.rem(s0, 2).astype(jnp.float32), lax.rem(s1, 2).astype(jnp.float32)
                a = raws[q][lax.div(s0, 2)].astype(jnp.float32)
                b = raws[q][lax.div(s1, 2)].astype(jnp.float32)
                cols = pl.ds(pl.multiple_of(r * sub, sub), sub)
                v = a * (low * (1.0 - e0)) + pltpu.roll(a, BLK, 1) * (low * e0)
                v += pltpu.roll(b, BLK, 1) * (high * (1.0 - e1)) + b * (high * e1)
                for i in range(per):
                    row = me * ext + q * per + i
                    w = v[i * BLK:(i + 1) * BLK] * keep(dpat[row, j], dpat[row, j + 1])
                    lbuf[c, pl.ds(q * sub + i * BLK, BLK), cols] = w.astype(jnp.bfloat16)

    def first(q, chunks):
        @pl.loop(0, width // NT)
        def _(t):
            cols = pl.ds(pl.multiple_of(t * NT, NT), NT)
            total = jnp.zeros((chunks * sub, NT), jnp.float32)
            for c in range(Q):
                h = hfull[:, pl.ds(c * sub, sub), cols].reshape(n * sub, NT)
                total += jnp.dot(lbuf[c, pl.ds(q * sub, chunks * sub), :], h, preferred_element_type=jnp.float32)
            for i in range(chunks):
                fbuf[q + i, me, :, cols] = total[i * sub:(i + 1) * sub].astype(jnp.bfloat16)

    def second(q):
        @pl.loop(0, width // NT)
        def _(t):
            cols = pl.ds(pl.multiple_of(t * NT, NT), NT)
            f = fbuf[q, :, :, cols].reshape(n * sub, NT)
            total = jnp.dot(lbuf[q], f, preferred_element_type=jnp.float32)
            if q > 0:
                total += out[:, cols]
            if q == Q - 1:
                own = fbuf[:, me, :, cols].reshape(rows, NT).astype(jnp.float32)
                total = 3.0 * own - 2.0 * total
            out[:, cols] = total

    gf = [
        Gather(
            (lambda q: lambda s, lo, size: fbuf.at[q, s, pl.ds(lo, size), :])(q),
            sub,
            (lambda q: lambda i: f_s.at[q, i])(q),
            (lambda q: lambda i: f_r.at[q, i])(q),
        )
        for q in range(Q)
    ]

    zown(0)
    zown(1)
    zstep(0, 1)
    gh.turn()
    for dist in range(2, m):
        zstep(0, dist)
    zown(2)
    zstep(1, 1)
    order(0)
    gh.share()
    for dist in range(2, m):
        zstep(1, dist)
    zown(3)
    zstep(2, 1)
    order(1)
    gh.finish()
    first(0, 2)
    gf[0].start()
    gf[1].start()
    for dist in range(2, m - 1):
        zstep(2, dist)
    zstep(3, 1)
    zstep(2, m - 1)
    gf[0].turn()
    order(2)
    first(2, 1)
    gf[2].start()
    gf[1].turn()
    for dist in range(2, m - 1):
        zstep(3, dist)
    gf[2].turn()
    zstep(3, m - 1)
    order(3)
    first(3, 1)
    gf[3].start()
    gf[0].share()
    gf[0].finish()
    second(0)
    gf[1].share()
    gf[1].finish()
    gf[3].turn()
    second(1)
    gf[2].share()
    gf[2].finish()
    gf[3].share()
    second(2)
    gf[3].finish()
    second(3)

    for c in migrants:
        c.wait_send()
    zdrain()
    gh.drain()
    for g in gf:
        g.drain()


def body(density, hamiltonian, density_pattern, ham_pattern, source):
    n, m = lax.axis_size("row"), lax.axis_size("col")
    rows, width = density.shape
    ext = rows // BLK
    sub = rows // Q
    sems = max(11, n - 1)
    dma = pltpu.SemaphoreType.DMA
    bf = jnp.bfloat16
    sm = pl.BlockSpec(memory_space=pltpu.SMEM)
    anywhere = pl.BlockSpec(memory_space=pl.ANY)
    vm = pl.BlockSpec(memory_space=pltpu.VMEM)
    return pl.pallas_call(
        functools.partial(kernel, n, m),
        out_shape=jax.ShapeDtypeStruct((rows, width), jnp.float32),
        in_specs=[sm, sm, sm, anywhere, anywhere],
        out_specs=vm,
        scratch_shapes=[
            pltpu.VMEM((ext, BLK, width), bf),
            pltpu.VMEM((rows, width), bf),
            pltpu.VMEM((ext + 2 * CAP, BLK, width), bf),
            pltpu.VMEM((2, CAP, BLK, width), bf),
            pltpu.VMEM((n, rows, width), bf),
            pltpu.VMEM((Q, rows, n * sub), bf),
            pltpu.VMEM((Q, n, sub, width), bf),
        ]
        + [pltpu.VMEM((m * width // (2 * BLK), sub, 2 * BLK), bf) for _ in range(Q)]
        + [
            dma((2,)), dma((2,)),
            dma((2, Q, m)), dma((2, Q, m)),
            dma((sems,)), dma((sems,)),
            dma((Q, sems)), dma((Q, sems)),
            dma((3,)),
        ],
        compiler_params=pltpu.CompilerParams(
            collective_id=0, has_side_effects=True, vmem_limit_bytes=60 * 1024 * 1024
        ),
        cost_estimate=pl.CostEstimate(
            flops=4 * rows * n * rows * width, bytes_accessed=8 * rows * width, transcendentals=0
        ),
    )(source, density_pattern, ham_pattern, density.reshape(ext, BLK, width), hamiltonian)


def solution(mesh):
    return jax.shard_map(
        body,
        mesh=mesh,
        in_specs=(P("row", "col"), P("row", "col"), P(), P(), P()),
        out_specs=P("row", "col"),
        check_vma=False,
    )
```

```python
import functools
import jax
import jax.numpy as jnp
from jax import lax
from jax.experimental import pallas as pl
from jax.experimental.pallas import tpu as pltpu
from jax.sharding import PartitionSpec as P

BLK = 64
CAP = 2
Q = 4
NT = 256
MESH = pl.DeviceIdType.MESH


def kernel(n, m, src, dpat, hpat, den_hbm, ham_hbm, out, den, ham, stack, pack, hfull, lbuf, fbuf, *rest):
    raws = rest[:Q]
    mig_s, mig_r, z_s, z_r, h_s, h_r, f_s, f_r, in_s = rest[Q:]
    me = lax.axis_index("row")
    zz = lax.axis_index("col")
    ext, _, width = den.shape
    rows = ext * BLK
    pairs = width // (2 * BLK)
    sub = rows // Q
    per = sub // BLK
    up, down = lax.rem(me + 1, n), lax.rem(me + n - 1, n)
    loads = [
        pltpu.make_async_copy(den_hbm, den, in_s.at[0]),
        pltpu.make_async_copy(ham_hbm, ham, in_s.at[1]),
        pltpu.make_async_copy(den_hbm, stack.at[pl.ds(0, ext)], in_s.at[2]),
    ]
    for c in loads:
        c.start()

    barrier = pltpu.get_barrier_semaphore()
    for p in range(1, n):
        pl.semaphore_signal(barrier, inc=1, device_id={"row": lax.rem(me + p, n)}, device_id_type=MESH)

    @pl.when(zz > 0)
    def _():
        pl.semaphore_signal(barrier, inc=1, device_id={"col": zz - 1}, device_id_type=MESH)

    @pl.when(zz < m - 1)
    def _():
        pl.semaphore_signal(barrier, inc=1, device_id={"col": zz + 1}, device_id_type=MESH)

    loads[0].wait()
    for side, target in enumerate((up, down)):
        count = jnp.int32(0)
        picks = [jnp.int32(0)] * CAP
        for i in range(ext):
            a = src[target * ext + i]
            hit = (lax.div(a, ext) == me).astype(jnp.int32)
            for k in range(CAP):
                picks[k] = picks[k] + hit * (count == k).astype(jnp.int32) * lax.rem(a, ext)
            count = count + hit
        for k in range(CAP):
            pack[side, k] = den[picks[k]]

    pl.semaphore_wait(barrier, n - 1 + (zz > 0).astype(jnp.int32) + (zz < m - 1).astype(jnp.int32))

    migrants = []
    for side, target in enumerate((up, down)):
        c = pltpu.make_async_remote_copy(
            src_ref=pack.at[side],
            dst_ref=stack.at[pl.ds(ext + side * CAP, CAP)],
            send_sem=mig_s.at[side],
            recv_sem=mig_r.at[side],
            device_id={"row": target},
            device_id_type=MESH,
        )
        c.start()
        migrants.append(c)

    loads[1].wait()
    lane = lax.broadcasted_iota(jnp.int32, (1, 2 * BLK), 1)
    low = (lane < BLK).astype(jnp.float32)
    high = 1.0 - low

    def keep(p0, p1):
        return low * p0.astype(jnp.float32) + high * p1.astype(jnp.float32)

    @pl.loop(0, ext, unroll=2)
    def _(i):
        for t in range(pairs):
            j = zz * pairs * 2 + t * 2
            s = pl.ds(pl.multiple_of(i * BLK, BLK), BLK)
            cols = pl.ds(t * 2 * BLK, 2 * BLK)
            row = me * ext + i
            w = ham[s, cols].astype(jnp.float32) * keep(hpat[row, j], hpat[row, j + 1])
            hfull[me, s, cols] = w.astype(jnp.bfloat16)

    loads[2].wait()

    class Gather:
        def __init__(self, view, size, ss, rs):
            self.view, self.size, self.ss, self.rs = view, size, ss, rs
            self.sent = []
            y, x, k = me // 4, lax.rem(me // 2, 2), lax.rem(me, 2)
            self.X = y * 4 + (1 - x) * 2 + k
            self.Y = (1 - y) * 4 + x * 2 + k
            self.D = (1 - y) * 4 + (1 - x) * 2 + k
            self.C = y * 4 + x * 2 + (1 - k)
            self.half = size // 2

        def other(self, slot):
            return slot + 1 - 2 * lax.rem(slot, 2)

        def copy(self, idx, slot, lo, size, target):
            return pltpu.make_async_remote_copy(
                src_ref=self.view(slot, lo, size),
                dst_ref=self.view(slot, lo, size),
                send_sem=self.ss(idx),
                recv_sem=self.rs(idx),
                device_id={"row": target},
                device_id_type=MESH,
            )

        def send(self, *args):
            c = self.copy(*args)
            c.start()
            self.sent.append(c)

        def recv(self, idx, slot, lo, size):
            self.copy(idx, slot, lo, size, self.other(me) if n == 8 else up).wait_recv()

        def start(self):
            h, size = self.half, self.size
            if n != 8:
                for p in range(1, n):
                    self.send(p - 1, me, 0, size, lax.rem(me + p, n))
                return
            self.send(0, me, 0, h, self.X)
            self.send(3, me, h, h, self.Y)
            self.send(1, me, h, h, self.X)
            self.send(2, me, 0, h, self.Y)
            self.send(6, me, 0, size, self.C)

        def turn(self):
            if n != 8:
                return
            h = self.half
            self.recv(0, self.X, 0, h)
            self.send(4, self.X, 0, h, self.Y)
            self.recv(3, self.Y, h, h)
            self.send(5, self.Y, h, h, self.X)

        def share(self):
            if n != 8:
                return
            h, size = self.half, self.size
            self.recv(1, self.X, h, h)
            self.send(7, self.X, 0, size, self.C)
            self.recv(2, self.Y, 0, h)
            self.send(8, self.Y, 0, size, self.C)

        def finish(self):
            h, size = self.half, self.size
            if n != 8:
                for p in range(1, n):
                    self.recv(p - 1, lax.rem(me + n - p, n), 0, size)
                return
            self.recv(4, self.D, 0, h)
            self.send(9, self.D, 0, h, self.C)
            self.recv(5, self.D, h, h)
            self.send(10, self.D, h, h, self.C)
            for idx, slot in ((6, self.C), (7, self.other(self.X)), (8, self.other(self.Y))):
                self.recv(idx, slot, 0, size)
            self.recv(9, self.other(self.D), 0, h)
            self.recv(10, self.other(self.D), h, h)

        def drain(self):
            for c in self.sent:
                c.wait_send()

    gh = Gather(lambda s, lo, size: hfull.at[s, pl.ds(lo, size), :], rows, lambda i: h_s.at[i], lambda i: h_r.at[i])
    gh.start()

    for c in migrants:
        c.wait_recv()
    nlow, nupp = jnp.int32(0), jnp.int32(0)
    for i in range(ext):
        a = src[me * ext + i]
        home = lax.div(a, ext)
        lower, upper = (home == down).astype(jnp.int32), (home == up).astype(jnp.int32)
        pick = lower * (ext + jnp.minimum(nlow, CAP - 1)) + upper * (ext + CAP + jnp.minimum(nupp, CAP - 1)) + (1 - lower - upper) * lax.rem(a, ext)
        nlow = nlow + lower
        nupp = nupp + upper
        block = stack[pick]
        for t in range(pairs):
            raws[i // per][zz * pairs + t, pl.ds((i % per) * BLK, BLK), :] = block[:, t * 2 * BLK:(t + 1) * 2 * BLK]

    def zcopy(d, q, dist, tile):
        ref = raws[q].at[pl.ds(tile * pairs, pairs)]
        return pltpu.make_async_remote_copy(
            src_ref=ref,
            dst_ref=ref,
            send_sem=z_s.at[d, q, dist],
            recv_sem=z_r.at[d, q, dist],
            device_id={"col": zz - 1 if d == 0 else zz + 1},
            device_id_type=MESH,
        )

    def zown(q):
        for d in range(2):
            @pl.when(zz > 0 if d == 0 else zz < m - 1)
            def _():
                zcopy(d, q, 0, zz).start()

    def zstep(q, dist):
        for d in range(2):
            tile = zz + dist if d == 0 else zz - dist
            there = tile < m if d == 0 else tile >= 0

            @pl.when(there)
            def _():
                zcopy(d, q, dist - 1, tile).wait_recv()

            if dist < m - 1:
                @pl.when(there & (zz > 0 if d == 0 else zz < m - 1))
                def _():
                    zcopy(d, q, dist, tile).start()

    def zdrain():
        for q in range(Q):
            for d in range(2):
                for dist in range(m - 1):
                    tile = zz + dist if d == 0 else zz - dist
                    there = (tile < m if d == 0 else tile >= 0) & (zz > 0 if d == 0 else zz < m - 1)

                    @pl.when(there)
                    def _():
                        zcopy(d, q, dist, tile).wait_send()

    def order(q):
        for c in range(Q):
            @pl.loop(0, n, unroll=4)
            def _(r):
                j = r * ext + c * per
                s0, s1 = src[j], src[j + 1]
                e0, e1 = lax.rem(s0, 2).astype(jnp.float32), lax.rem(s1, 2).astype(jnp.float32)
                a = raws[q][lax.div(s0, 2)].astype(jnp.float32)
                b = raws[q][lax.div(s1, 2)].astype(jnp.float32)
                cols = pl.ds(pl.multiple_of(r * sub, sub), sub)
                v = a * (low * (1.0 - e0)) + pltpu.roll(a, BLK, 1) * (low * e0)
                v += pltpu.roll(b, BLK, 1) * (high * (1.0 - e1)) + b * (high * e1)
                for i in range(per):
                    row = me * ext + q * per + i
                    w = v[i * BLK:(i + 1) * BLK] * keep(dpat[row, j], dpat[row, j + 1])
                    lbuf[c, pl.ds(q * sub + i * BLK, BLK), cols] = w.astype(jnp.bfloat16)

    def first(q, chunks):
        @pl.loop(0, width // NT)
        def _(t):
            cols = pl.ds(pl.multiple_of(t * NT, NT), NT)
            total = jnp.zeros((chunks * sub, NT), jnp.float32)
            for c in range(Q):
                h = hfull[:, pl.ds(c * sub, sub), cols].reshape(n * sub, NT)
                total += jnp.dot(lbuf[c, pl.ds(q * sub, chunks * sub), :], h, preferred_element_type=jnp.float32)
            for i in range(chunks):
                fbuf[q + i, me, :, cols] = total[i * sub:(i + 1) * sub].astype(jnp.bfloat16)

    def second(q):
        @pl.loop(0, width // NT)
        def _(t):
            cols = pl.ds(pl.multiple_of(t * NT, NT), NT)
            f = fbuf[q, :, :, cols].reshape(n * sub, NT)
            total = jnp.dot(lbuf[q], f, preferred_element_type=jnp.float32)
            if q > 0:
                total += out[:, cols]
            if q == Q - 1:
                own = fbuf[:, me, :, cols].reshape(rows, NT).astype(jnp.float32)
                total = 3.0 * own - 2.0 * total
            out[:, cols] = total

    gf = [
        Gather(
            (lambda q: lambda s, lo, size: fbuf.at[q, s, pl.ds(lo, size), :])(q),
            sub,
            (lambda q: lambda i: f_s.at[q, i])(q),
            (lambda q: lambda i: f_r.at[q, i])(q),
        )
        for q in range(Q)
    ]

    zown(0)
    zown(1)
    zstep(0, 1)
    gh.turn()
    for dist in range(2, m):
        zstep(0, dist)
    zown(2)
    zstep(1, 1)
    order(0)
    gh.share()
    for dist in range(2, m):
        zstep(1, dist)
    zown(3)
    zstep(2, 1)
    order(1)
    gh.finish()
    first(0, 2)
    gf[0].start()
    gf[1].start()
    for dist in range(2, m - 1):
        zstep(2, dist)
    zstep(3, 1)
    zstep(2, m - 1)
    gf[0].turn()
    order(2)
    first(2, 1)
    gf[2].start()
    gf[1].turn()
    for dist in range(2, m - 1):
        zstep(3, dist)
    gf[2].turn()
    zstep(3, m - 1)
    order(3)
    first(3, 1)
    gf[3].start()
    gf[0].share()
    gf[0].finish()
    second(0)
    gf[1].share()
    gf[1].finish()
    gf[3].turn()
    second(1)
    gf[2].share()
    gf[2].finish()
    gf[3].share()
    second(2)
    gf[3].finish()
    second(3)

    for c in migrants:
        c.wait_send()
    zdrain()
    gh.drain()
    for g in gf:
        g.drain()


def body(density, hamiltonian, density_pattern, ham_pattern, source):
    n, m = lax.axis_size("row"), lax.axis_size("col")
    rows, width = density.shape
    ext = rows // BLK
    sub = rows // Q
    sems = max(11, n - 1)
    dma = pltpu.SemaphoreType.DMA
    bf = jnp.bfloat16
    sm = pl.BlockSpec(memory_space=pltpu.SMEM)
    anywhere = pl.BlockSpec(memory_space=pl.ANY)
    vm = pl.BlockSpec(memory_space=pltpu.VMEM)
    return pl.pallas_call(
        functools.partial(kernel, n, m),
        out_shape=jax.ShapeDtypeStruct((rows, width), jnp.float32),
        in_specs=[sm, sm, sm, anywhere, anywhere],
        out_specs=vm,
        scratch_shapes=[
            pltpu.VMEM((ext, BLK, width), bf),
            pltpu.VMEM((rows, width), bf),
            pltpu.VMEM((ext + 2 * CAP, BLK, width), bf),
            pltpu.VMEM((2, CAP, BLK, width), bf),
            pltpu.VMEM((n, rows, width), bf),
            pltpu.VMEM((Q, rows, n * sub), bf),
            pltpu.VMEM((Q, n, sub, width), bf),
        ]
        + [pltpu.VMEM((m * width // (2 * BLK), sub, 2 * BLK), bf) for _ in range(Q)]
        + [
            dma((2,)), dma((2,)),
            dma((2, Q, m)), dma((2, Q, m)),
            dma((sems,)), dma((sems,)),
            dma((Q, sems)), dma((Q, sems)),
            dma((3,)),
        ],
        compiler_params=pltpu.CompilerParams(
            collective_id=0, has_side_effects=True, vmem_limit_bytes=60 * 1024 * 1024
        ),
        cost_estimate=pl.CostEstimate(
            flops=4 * rows * n * rows * width, bytes_accessed=8 * rows * width, transcendentals=0
        ),
    )(source, density_pattern, ham_pattern, density.reshape(ext, BLK, width), hamiltonian)


def solution(mesh):
    return jax.shard_map(
        body,
        mesh=mesh,
        in_specs=(P("row", "col"), P("row", "col"), P(), P(), P()),
        out_specs=P("row", "col"),
        check_vma=False,
    )
```
